32 devices in a mesh: grp: 2 (over y), chan: 2 (over x), tm: 4 (over z), pol: 2 (over core).
Axes of the slice: x: 2, y: 2, z: 4, core: 2. Of those that a mesh axis runs over, the one named last changes fastest.
Arguments:
- voltages: bfloat16 [4, 2, 256, 32768], P('grp', 'pol', 'chan', 'tm'), parts along dimension 0, may hold values from -6 to 6
- taps_filter: float32 [16, 2048], replicated, may hold values from -1.5 to 1.5
- tile_a: int32 [14, 64], replicated, may hold values from 0 to 255
- tile_b: int32 [14, 64], replicated, may hold values from 0 to 255
- tile_owner: int32 [14], replicated, may hold values from 0 to 1, as said below
- tile_flags: int32 [14, 16], replicated, may hold values 0 or 1
Outputs:
- visibility: float32 [16, 256, 4, 2, 64, 128], P('pol', ('chan', 'tm'), 'grp'), parts along dimension 2
The draws below stay inside these ranges and needn't reach their ends.
There are 2 independent parts, one for each index of `grp`. The reference program is written for one: setup_inputs(seed, part) draws one part's arguments, and reference() takes and returns one part's arrays. A program takes and returns all parts, laid end to end along the dimension named above; an argument that names none is the same for every part. Nothing has to cross between parts.
Inputs may be any that keep to these rules, and one draw needn't show every extreme that they name: `tile_owner`: one owner holds exactly 8 tiles and the other owner holds all the rest.
All inputs are finite; a program needn't handle non-finite values.
Results may differ from the reference program's by a relative error of at most 0.0035.
Values may be sent and summed in bfloat16 or wider, within the bound.
A program may use at most 128 MiB of HBM per device.

```python
import math
import jax
import jax.numpy as jnp
from jax import lax

S = 256
C = 2048
TAPS = 16
AVG = 8
TS = 64
NTILE = 14
CAP = 8
T_SIZE = 16
GROUPS = 256
N_POL = 2


def draw_tile_owner(key, part):
    heavier = jax.random.randint(jax.random.fold_in(key, 11), (), 0, 2)
    order = jax.random.permutation(jax.random.fold_in(key, 12), NTILE)
    ranked = jnp.where(jnp.arange(NTILE) < CAP, heavier, 1 - heavier)
    return jnp.take(ranked, order).astype(jnp.int32)


def set_ends(drawn, key, least, largest):
    spot = [jax.random.randint(jax.random.fold_in(key, axis), (), 0, length) for axis, length in enumerate(drawn.shape)]
    longest = drawn.shape.index(max(drawn.shape))
    neighbour = spot[:longest] + [(spot[longest] + 1) % drawn.shape[longest]] + spot[longest + 1:]
    return drawn.at[tuple(spot)].set(least).at[tuple(neighbour)].set(largest)


def block_scale(key, extent, shards, smallest, high):
    gain, own = 1.0, jax.random.fold_in(key, 6)
    for axis_at, blocks in shards:
        steps = jnp.exp(jax.random.uniform(jax.random.fold_in(own, axis_at), (blocks,), jnp.float32, smallest / len(shards), high / len(shards)))
        gain = gain * jnp.repeat(steps, extent[axis_at] // blocks).reshape([-1 if axis == axis_at else 1 for axis in range(len(extent))])
    return gain


def noise(own_key, dims, deviation, limit, split=(), held_as=jnp.bfloat16):
    values = deviation * jax.random.normal(own_key, dims, jnp.float32)
    if split:
        values = values * block_scale(own_key, dims, split, -0.22, 0.18)
    return jnp.clip(values, -limit, limit).astype(held_as)


def setup_inputs(seed: int = 0, part: int = 0) -> dict:
    key_of = jax.random.split(jax.random.key(seed), 7)
    part_keys = jax.random.split(jax.random.fold_in(key_of[6], part), 7)
    return {
        "voltages": noise(part_keys[0], (2, 2, S, T_SIZE * C), 1.0, 6.0, ((1, 2), (2, 2), (3, 4))),
        "taps_filter": noise(key_of[1], (TAPS, C), TAPS ** -0.5, 1.5, (), jnp.float32),
        "tile_a": set_ends(jax.random.randint(key_of[2], (NTILE, TS), 0, S), jax.random.fold_in(key_of[2], 1), 0, S - 1).astype(jnp.int32),
        "tile_b": set_ends(jax.random.randint(key_of[3], (NTILE, TS), 0, S), jax.random.fold_in(key_of[3], 1), 0, S - 1).astype(jnp.int32),
        "tile_owner": draw_tile_owner(jax.random.fold_in(key_of[6], 71), part),
        "tile_flags": set_ends((jax.random.randint(key_of[5], (NTILE, T_SIZE), 0, 4) < 3).astype(jnp.int32), jax.random.fold_in(key_of[5], 1), 0, 1),
    }


def station_spectra(samples, taps_filter):
    blocks = samples.astype(jnp.float32).reshape(2, 2, T_SIZE, C)
    padded = jnp.pad(blocks, ((0, 0), (0, 0), (TAPS - 1, 0), (0, 0)))
    filtered = jnp.zeros((2, 2, T_SIZE, C), jnp.float32)
    for tap_index in range(TAPS):
        start = TAPS - 1 - tap_index
        filtered = filtered + taps_filter[tap_index] * padded[:, :, start:start + T_SIZE]
    transformed = jnp.fft.fft(filtered[0] + 1j * filtered[1], axis=-1) / math.sqrt(C)
    return jnp.stack([jnp.real(transformed), jnp.imag(transformed)]).astype(jnp.bfloat16)

def tile_result(arranged, rows_a, rows_b, flags):
    weight = jnp.tile(flags.astype(jnp.bfloat16), AVG)
    left_rows = (jnp.take(arranged, rows_a, axis=2) * weight).astype(jnp.float32)
    right_rows = jnp.take(arranged, rows_b, axis=2).astype(jnp.float32)
    exact_mode = lax.Precision.HIGHEST
    form = 'pank,qbnk->npaqb'
    real_part = jnp.einsum(form, left_rows[0], right_rows[0], precision=exact_mode) + jnp.einsum(form, left_rows[1], right_rows[1], precision=exact_mode)
    imag_part = jnp.einsum(form, left_rows[1], right_rows[0], precision=exact_mode) - jnp.einsum(form, left_rows[0], right_rows[1], precision=exact_mode)
    result = jnp.stack([real_part, imag_part], axis=1) * (1.0 / (AVG * T_SIZE))
    return result.reshape(GROUPS, 2, 2, TS, 2 * TS)

def reference(voltages, taps_filter, tile_a, tile_b, tile_owner, tile_flags):
    by_station = jnp.moveaxis(voltages, 2, 0)
    spectra = lax.map(lambda samples: station_spectra(samples, taps_filter), by_station)
    arranged = spectra.reshape(S, 2, 2, T_SIZE, GROUPS, AVG)
    arranged = arranged.transpose(1, 2, 0, 4, 5, 3).reshape(2, 2, S, GROUPS, AVG * T_SIZE)
    tile_results = lax.map(lambda items: tile_result(arranged, items[0], items[1], items[2]), (tile_a, tile_b, tile_flags))
    slots = []
    for holder in range(N_POL):
        chosen = tile_owner == holder
        listed = jnp.nonzero(chosen, size=CAP, fill_value=0)[0].astype(jnp.int32)
        tally = jnp.sum(chosen.astype(jnp.int32))
        active = jnp.arange(CAP, dtype=jnp.int32) < tally
        picked = jnp.take(tile_results, listed, axis=0)
        slots.append(jnp.where(active[:, None, None, None, None, None], picked, jnp.zeros_like(picked)))
    return jnp.concatenate(slots, axis=0)
```

```python
import math

import jax
import jax.numpy as jnp
from jax import lax
from jax.experimental import pallas as pl
from jax.experimental.pallas import tpu as pltpu
from jax.sharding import PartitionSpec as P

AVG = 8
CAP = 8

radix_first = 16


def fourier(filtered):
    length = filtered.shape[-1]
    second = length // radix_first
    mode = lax.Precision.HIGH
    grid = filtered.reshape(filtered.shape[:-1] + (radix_first, second))
    outer = jnp.arange(radix_first, dtype=jnp.int32)
    inner = jnp.arange(second, dtype=jnp.int32)
    phase_one = (
        2.0
        * math.pi
        / radix_first
        * (outer[:, None] * outer[None, :] % radix_first).astype(jnp.float32)
    )
    phase_twist = 2.0 * math.pi / length * (outer[:, None] * inner[None, :]).astype(jnp.float32)
    phase_two = (
        2.0 * math.pi / second * (inner[:, None] * inner[None, :] % second).astype(jnp.float32)
    )
    scale = 1.0 / math.sqrt(length)
    cos_one, sin_one = (jnp.cos(phase_one), jnp.sin(phase_one))
    cos_twist, sin_twist = (jnp.cos(phase_twist), jnp.sin(phase_twist))
    cos_two, sin_two = (jnp.cos(phase_two) * scale, jnp.sin(phase_two) * scale)
    one = jnp.stack([jnp.stack([cos_one, sin_one]), jnp.stack([-sin_one, cos_one])])
    two = jnp.stack([jnp.stack([cos_two, sin_two]), jnp.stack([-sin_two, cos_two])])
    section = jnp.einsum("qrfk,rnkj->qnfj", one, grid, precision=mode)
    turned = jnp.stack(
        [
            section[0] * cos_twist + section[1] * sin_twist,
            section[1] * cos_twist - section[0] * sin_twist,
        ]
    )
    return jnp.einsum("qrgj,rnfj->qngf", two, turned, precision=mode)


def correlate_kernel(bands, stations, rows_ref, weight_ref, full_ref, out_ref):
    width = rows_ref.shape[1] // 2
    depth = full_ref.shape[-1]
    columns = lax.broadcasted_iota(jnp.int32, (2 * width, stations), 1)
    pick = jnp.where(rows_ref[0] == columns, 1.0, 0.0).astype(jnp.bfloat16)
    weight = weight_ref[0]
    for band in range(bands):
        source = jnp.concatenate(
            [
                full_ref[p, :, band, r].reshape(stations, depth)
                for p in range(2)
                for r in range(2)
            ],
            axis=-1,
        )
        picked = jnp.dot(pick, source, preferred_element_type=jnp.float32)
        parts = [picked[:, i * depth : (i + 1) * depth] for i in range(4)]
        left = [part[:width] * weight for part in parts]
        right = [part[width:] for part in parts]
        left_rows = jnp.concatenate(
            [
                jnp.concatenate([left[0], left[1]], axis=-1),
                jnp.concatenate([left[2], left[3]], axis=-1),
                jnp.concatenate([left[1], -left[0]], axis=-1),
                jnp.concatenate([left[3], -left[2]], axis=-1),
            ],
            axis=0,
        ).astype(jnp.bfloat16)
        right_rows = jnp.concatenate(
            [
                jnp.concatenate([right[0], right[1]], axis=-1),
                jnp.concatenate([right[2], right[3]], axis=-1),
            ],
            axis=0,
        ).astype(jnp.bfloat16)
        result = lax.dot_general(
            left_rows,
            right_rows,
            (((1,), (1,)), ((), ())),
            preferred_element_type=jnp.float32,
        ) * (1.0 / depth)
        out_ref[0, band] = result.reshape(2, 2, width, 2 * width)


def correlate(full, rows, weight):
    pols, sources, bands, parts, part_stations, depth = full.shape
    width = rows.shape[1] // 2
    step = 4 if bands % 4 == 0 else 1
    return pl.pallas_call(
        lambda *refs: correlate_kernel(step, sources * part_stations, *refs),
        grid=(bands // step, CAP),
        in_specs=[
            pl.BlockSpec((1, 2 * width, 1), lambda g, n: (n, 0, 0)),
            pl.BlockSpec((1, 1, depth), lambda g, n: (n, 0, 0)),
            pl.BlockSpec(
                (pols, sources, step, parts, part_stations, depth), lambda g, n: (0, 0, g, 0, 0, 0)
            ),
        ],
        out_specs=pl.BlockSpec(
            (1, step, 2, 2, width, 2 * width), lambda g, n: (n, g, 0, 0, 0, 0)
        ),
        out_shape=jax.ShapeDtypeStruct((CAP, bands, 2, 2, width, 2 * width), jnp.float32),
        compiler_params=pltpu.CompilerParams(vmem_limit_bytes=48 * 2**20),
    )(rows, weight, full)


def on_device(voltages, taps_filter, tile_a, tile_b, tile_owner, tile_flags):
    taps, length = taps_filter.shape
    stations = voltages.shape[2]
    frames = voltages.shape[3] // length
    chan_count = lax.axis_size("chan")
    time_count = lax.axis_size("tm")
    spectra_count = time_count * frames
    share = stations // time_count

    blocks = voltages.reshape(2, time_count, share, frames * length)
    blocks = lax.all_to_all(blocks, "tm", split_axis=1, concat_axis=1, tiled=True)
    blocks = blocks.reshape(2, time_count, share, frames, length)
    blocks = blocks.transpose(0, 2, 1, 3, 4).reshape(2, share, spectra_count, length)
    extended = jnp.pad(blocks, ((0, 0), (0, 0), (taps - 1, 0), (0, 0)))
    filtered = jnp.zeros((2, share, spectra_count, length), jnp.float32)
    for tap_index in range(taps):
        start = taps - 1 - tap_index
        filtered = filtered + taps_filter[tap_index] * extended[
            :, :, start : start + spectra_count
        ].astype(jnp.float32)
    spectra = fourier(filtered.reshape(2, share * spectra_count, length)).astype(jnp.bfloat16)

    owners = chan_count * time_count
    bands = length // (owners * AVG)
    outgoing = spectra.reshape(2, share, spectra_count, owners, bands, AVG)
    outgoing = outgoing.transpose(3, 4, 0, 1, 5, 2).reshape(
        owners, bands, 2, share, AVG * spectra_count
    )
    moved = lax.all_to_all(outgoing, ("chan", "tm"), split_axis=0, concat_axis=0, tiled=True)
    full = lax.all_gather(moved, "pol", axis=0)

    position = lax.axis_index("pol")
    held = tile_owner == position
    rank = jnp.cumsum(held.astype(jnp.int32)) - 1
    chosen = (
        (rank[None, :] == jnp.arange(CAP, dtype=jnp.int32)[:, None]) & held[None, :]
    ).astype(jnp.int32)
    pairs = jnp.concatenate([tile_a, tile_b], axis=1)
    rows = jnp.sum(chosen[:, :, None] * pairs[None], axis=1)[:, :, None]
    flags = jnp.sum(chosen[:, :, None] * tile_flags[None], axis=1)
    weight = jnp.tile(flags.astype(jnp.float32), (1, AVG))[:, None, :]
    return correlate(full, rows, weight)


def solution(mesh):
    return jax.shard_map(
        on_device,
        mesh=mesh,
        in_specs=(P("grp", "pol", "chan", "tm"), P(), P(), P(), P(), P()),
        out_specs=P("pol", ("chan", "tm"), "grp", None, None, None),
        check_vma=False,
    )
```

```python
import math

import jax
import ml_dtypes
import numpy as np
import jax.numpy as jnp
from jax import lax
from jax.experimental import pallas as pl
from jax.experimental.pallas import tpu as pltpu
from jax.sharding import PartitionSpec as P

AVG = 8
CAP = 8

radix_first = 16


def fourier(filtered):
    length = filtered.shape[-1]
    second = length // radix_first
    mode = lax.Precision.HIGH
    grid = filtered.reshape(filtered.shape[:-1] + (radix_first, second))
    outer = jnp.arange(radix_first, dtype=jnp.int32)
    inner = jnp.arange(second, dtype=jnp.int32)
    phase_one = (
        2.0
        * math.pi
        / radix_first
        * (outer[:, None] * outer[None, :] % radix_first).astype(jnp.float32)
    )
    phase_twist = 2.0 * math.pi / length * (outer[:, None] * inner[None, :]).astype(jnp.float32)
    phase_two = (
        2.0 * math.pi / second * (inner[:, None] * inner[None, :] % second).astype(jnp.float32)
    )
    scale = 1.0 / math.sqrt(length)
    cos_one, sin_one = (jnp.cos(phase_one), jnp.sin(phase_one))
    cos_twist, sin_twist = (jnp.cos(phase_twist), jnp.sin(phase_twist))
    cos_two, sin_two = (jnp.cos(phase_two) * scale, jnp.sin(phase_two) * scale)
    one = jnp.stack([jnp.stack([cos_one, sin_one]), jnp.stack([-sin_one, cos_one])])
    two = jnp.stack([jnp.stack([cos_two, sin_two]), jnp.stack([-sin_two, cos_two])])
    section = jnp.einsum("qrfk,rnkj->qnfj", one, grid, precision=mode)
    turned = jnp.stack(
        [
            section[0] * cos_twist + section[1] * sin_twist,
            section[1] * cos_twist - section[0] * sin_twist,
        ]
    )
    return jnp.einsum("qrgj,rnfj->qngf", two, turned, precision=mode)


def times(value, angle):
    re, im = value
    if angle % 16 == 0:
        return re, im
    c, s = math.cos(2.0 * math.pi * angle / 16), math.sin(2.0 * math.pi * angle / 16)
    if angle % 16 == 4:
        return im, -re
    return re * c + im * s, im * c - re * s


def four(x):
    plus = [x[0][i] + x[2][i] for i in range(2)]
    minus = [x[0][i] - x[2][i] for i in range(2)]
    plus_odd = [x[1][i] + x[3][i] for i in range(2)]
    minus_odd = [x[1][i] - x[3][i] for i in range(2)]
    return [
        (plus[0] + plus_odd[0], plus[1] + plus_odd[1]),
        (minus[0] + minus_odd[1], minus[1] - minus_odd[0]),
        (plus[0] - plus_odd[0], plus[1] - plus_odd[1]),
        (minus[0] - minus_odd[1], minus[1] + minus_odd[0]),
    ]


def sixteen(x):
    inner = [four([x[4 * a + b] for a in range(4)]) for b in range(4)]
    result = [None] * 16
    for c in range(4):
        ends = four([times(inner[b][c], b * c) for b in range(4)])
        for d in range(4):
            result[c + 4 * d] = ends[d]
    return result


def spectra_kernel(x_ref, taps_ref, cos_ref, sin_ref, high_ref, low_ref, out_ref, held, turned):
    time_count, block = x_ref.shape[1:3]
    taps, length = taps_ref.shape
    frames = x_ref.shape[3] // length
    spectra_count = time_count * frames
    second = length // radix_first
    depth = AVG * spectra_count

    def filter_section(k1, carry):
        at = pl.multiple_of(k1 * second, second)
        rows = [taps_ref[m : m + 1, pl.ds(at, second)] for m in range(taps)]
        for r in range(2):
            samples = []
            for t in range(spectra_count):
                place = pl.multiple_of(k1 * second + (t % frames) * length, second)
                samples.append(x_ref[r, t // frames, :, pl.ds(place, second)].astype(jnp.float32))
            filtered = []
            for t in range(spectra_count):
                total = rows[0] * samples[t]
                for m in range(1, min(taps, t + 1)):
                    total = total + rows[m] * samples[t - m]
                filtered.append(total)
            held[r, :, :, pl.ds(at, second)] = jnp.transpose(jnp.stack(filtered), (1, 0, 2))
        return carry

    lax.fori_loop(0, radix_first, filter_section, 0)

    def transform_station(s, carry):
        sections = [
            tuple(held[r, s, :, k1 * second : (k1 + 1) * second] for r in range(2))
            for k1 in range(radix_first)
        ]
        rows = []
        for f1, (re, im) in enumerate(sixteen(sections)):
            c, n = cos_ref[f1 : f1 + 1, :], sin_ref[f1 : f1 + 1, :]
            rows.append(jnp.concatenate([re * c + im * n, im * c - re * n], axis=-1))
        joined = jnp.concatenate(rows, axis=0)
        high = joined.astype(jnp.bfloat16)
        low = (joined - high.astype(jnp.float32)).astype(jnp.bfloat16)

        def product(matrix, data):
            return lax.dot_general(
                matrix, data, (((1,), (1,)), ((), ())), preferred_element_type=jnp.float32
            )

        turned[s] = (
            product(high_ref[...], high)
            + product(high_ref[...], low)
            + product(low_ref[...], high)
        )
        return carry

    lax.fori_loop(0, block, transform_station, 0)

    def place_channels(f, carry):
        at = pl.multiple_of(f * 16, 16)
        for q in range(2):
            for h in range(radix_first // AVG):
                part = turned[:, pl.ds(q * second + at, 16), h * depth : (h + 1) * depth]
                out_ref[pl.ds(at, 16), h, q] = jnp.transpose(part, (1, 0, 2)).astype(jnp.bfloat16)
        return carry

    lax.fori_loop(0, second // 16, place_channels, 0)


def local_spectra(blocks, taps_filter):
    _, time_count, share, samples = blocks.shape
    taps, length = taps_filter.shape
    spectra_count = time_count * (samples // length)
    second = length // radix_first
    depth = AVG * spectra_count
    block = 16
    inner = np.arange(second)
    twist = 2.0 * np.pi / length * (np.arange(radix_first)[:, None] * inner[None, :])
    phase = 2.0 * np.pi / second * (inner[:, None] * inner[None, :] % second)
    c, s = np.cos(phase) / math.sqrt(length), np.sin(phase) / math.sqrt(length)
    matrix = np.block([[c, s], [-s, c]])
    high = matrix.astype(ml_dtypes.bfloat16)
    low = (matrix - high.astype(np.float64)).astype(ml_dtypes.bfloat16)
    whole = lambda shape: pl.BlockSpec(shape, lambda i: (0, 0))
    return pl.pallas_call(
        spectra_kernel,
        grid=(share // block,),
        in_specs=[
            pl.BlockSpec((2, time_count, block, samples), lambda i: (0, 0, i, 0)),
            whole((taps, length)),
            whole((radix_first, second)),
            whole((radix_first, second)),
            whole((2 * second, 2 * second)),
            whole((2 * second, 2 * second)),
        ],
        out_specs=pl.BlockSpec(
            (second, radix_first // AVG, 2, block, depth), lambda i: (0, 0, 0, i, 0)
        ),
        out_shape=jax.ShapeDtypeStruct(
            (second, radix_first // AVG, 2, share, depth), jnp.bfloat16
        ),
        scratch_shapes=[
            pltpu.VMEM((2, block, spectra_count, length), jnp.float32),
            pltpu.VMEM((block, 2 * second, radix_first * spectra_count), jnp.float32),
        ],
        compiler_params=pltpu.CompilerParams(vmem_limit_bytes=48 * 2**20),
    )(
        blocks,
        taps_filter,
        np.cos(twist).astype(np.float32),
        np.sin(twist).astype(np.float32),
        high,
        low,
    )


def plain_spectra(blocks, taps_filter):
    _, time_count, share, samples = blocks.shape
    taps, length = taps_filter.shape
    frames = samples // length
    spectra_count = time_count * frames
    blocks = blocks.reshape(2, time_count, share, frames, length)
    blocks = blocks.transpose(0, 2, 1, 3, 4).reshape(2, share, spectra_count, length)
    extended = jnp.pad(blocks, ((0, 0), (0, 0), (taps - 1, 0), (0, 0)))
    filtered = jnp.zeros((2, share, spectra_count, length), jnp.float32)
    for tap_index in range(taps):
        start = taps - 1 - tap_index
        filtered = filtered + taps_filter[tap_index] * extended[
            :, :, start : start + spectra_count
        ].astype(jnp.float32)
    spectra = fourier(filtered.reshape(2, share * spectra_count, length)).astype(jnp.bfloat16)
    outgoing = spectra.reshape(
        2, share, spectra_count, length // radix_first, radix_first // AVG, AVG
    )
    return outgoing.transpose(3, 4, 0, 1, 5, 2).reshape(
        length // radix_first, radix_first // AVG, 2, share, AVG * spectra_count
    )


def correlate_kernel(bands, stations, rows_ref, weight_ref, full_ref, out_ref):
    width = rows_ref.shape[1] // 2
    depth = full_ref.shape[-1]
    columns = lax.broadcasted_iota(jnp.int32, (2 * width, stations), 1)
    pick = jnp.where(rows_ref[0] == columns, 1.0, 0.0).astype(jnp.bfloat16)
    weight = weight_ref[0]
    for band in range(bands):
        source = jnp.concatenate(
            [
                full_ref[p, :, band, r].reshape(stations, depth)
                for p in range(2)
                for r in range(2)
            ],
            axis=-1,
        )
        picked = jnp.dot(pick, source, preferred_element_type=jnp.float32)
        parts = [picked[:, i * depth : (i + 1) * depth] for i in range(4)]
        left = [part[:width] * weight for part in parts]
        right = [part[width:] for part in parts]
        left_rows = jnp.concatenate(
            [
                jnp.concatenate([left[0], left[1]], axis=-1),
                jnp.concatenate([left[2], left[3]], axis=-1),
                jnp.concatenate([left[1], -left[0]], axis=-1),
                jnp.concatenate([left[3], -left[2]], axis=-1),
            ],
            axis=0,
        ).astype(jnp.bfloat16)
        right_rows = jnp.concatenate(
            [
                jnp.concatenate([right[0], right[1]], axis=-1),
                jnp.concatenate([right[2], right[3]], axis=-1),
            ],
            axis=0,
        ).astype(jnp.bfloat16)
        result = lax.dot_general(
            left_rows,
            right_rows,
            (((1,), (1,)), ((), ())),
            preferred_element_type=jnp.float32,
        ) * (1.0 / depth)
        out_ref[0, band] = result.reshape(2, 2, width, 2 * width)


def correlate(full, rows, weight):
    pols, sources, bands, parts, part_stations, depth = full.shape
    width = rows.shape[1] // 2
    step = 4 if bands % 4 == 0 else 1
    return pl.pallas_call(
        lambda *refs: correlate_kernel(step, sources * part_stations, *refs),
        grid=(bands // step, CAP),
        in_specs=[
            pl.BlockSpec((1, 2 * width, 1), lambda g, n: (n, 0, 0)),
            pl.BlockSpec((1, 1, depth), lambda g, n: (n, 0, 0)),
            pl.BlockSpec(
                (pols, sources, step, parts, part_stations, depth), lambda g, n: (0, 0, g, 0, 0, 0)
            ),
        ],
        out_specs=pl.BlockSpec(
            (1, step, 2, 2, width, 2 * width), lambda g, n: (n, g, 0, 0, 0, 0)
        ),
        out_shape=jax.ShapeDtypeStruct((CAP, bands, 2, 2, width, 2 * width), jnp.float32),
        compiler_params=pltpu.CompilerParams(vmem_limit_bytes=48 * 2**20),
    )(rows, weight, full)


def on_device(voltages, taps_filter, tile_a, tile_b, tile_owner, tile_flags):
    taps, length = taps_filter.shape
    stations = voltages.shape[2]
    frames = voltages.shape[3] // length
    chan_count = lax.axis_size("chan")
    time_count = lax.axis_size("tm")
    spectra_count = time_count * frames
    share = stations // time_count

    blocks = voltages.reshape(2, time_count, share, frames * length)
    blocks = lax.all_to_all(blocks, "tm", split_axis=1, concat_axis=1, tiled=True)
    spectra = (local_spectra if share % 16 == 0 else plain_spectra)(blocks, taps_filter)

    owners = chan_count * time_count
    bands = length // (owners * AVG)
    outgoing = spectra.reshape(owners, bands, 2, share, AVG * spectra_count)
    moved = lax.all_to_all(outgoing, ("chan", "tm"), split_axis=0, concat_axis=0, tiled=True)
    full = lax.all_gather(moved, "pol", axis=0)

    position = lax.axis_index("pol")
    held = tile_owner == position
    rank = jnp.cumsum(held.astype(jnp.int32)) - 1
    chosen = (
        (rank[None, :] == jnp.arange(CAP, dtype=jnp.int32)[:, None]) & held[None, :]
    ).astype(jnp.int32)
    pairs = jnp.concatenate([tile_a, tile_b], axis=1)
    rows = jnp.sum(chosen[:, :, None] * pairs[None], axis=1)[:, :, None]
    flags = jnp.sum(chosen[:, :, None] * tile_flags[None], axis=1)
    weight = jnp.tile(flags.astype(jnp.float32), (1, AVG))[:, None, :]
    return correlate(full, rows, weight)


def solution(mesh):
    return jax.shard_map(
        on_device,
        mesh=mesh,
        in_specs=(P("grp", "pol", "chan", "tm"), P(), P(), P(), P(), P()),
        out_specs=P("pol", ("chan", "tm"), "grp", None, None, None),
        check_vma=False,
    )
```

```python
import math

import jax
import ml_dtypes
import numpy as np
import jax.numpy as jnp
from jax import lax
from jax.experimental import pallas as pl
from jax.experimental.pallas import tpu as pltpu
from jax.sharding import PartitionSpec as P

AVG = 8
CAP = 8

radix_first = 16


def fourier(filtered):
    length = filtered.shape[-1]
    second = length // radix_first
    mode = lax.Precision.HIGH
    grid = filtered.reshape(filtered.shape[:-1] + (radix_first, second))
    outer = jnp.arange(radix_first, dtype=jnp.int32)
    inner = jnp.arange(second, dtype=jnp.int32)
    phase_one = (
        2.0
        * math.pi
        / radix_first
        * (outer[:, None] * outer[None, :] % radix_first).astype(jnp.float32)
    )
    phase_twist = 2.0 * math.pi / length * (outer[:, None] * inner[None, :]).astype(jnp.float32)
    phase_two = (
        2.0 * math.pi / second * (inner[:, None] * inner[None, :] % second).astype(jnp.float32)
    )
    scale = 1.0 / math.sqrt(length)
    cos_one, sin_one = (jnp.cos(phase_one), jnp.sin(phase_one))
    cos_twist, sin_twist = (jnp.cos(phase_twist), jnp.sin(phase_twist))
    cos_two, sin_two = (jnp.cos(phase_two) * scale, jnp.sin(phase_two) * scale)
    one = jnp.stack([jnp.stack([cos_one, sin_one]), jnp.stack([-sin_one, cos_one])])
    two = jnp.stack([jnp.stack([cos_two, sin_two]), jnp.stack([-sin_two, cos_two])])
    section = jnp.einsum("qrfk,rnkj->qnfj", one, grid, precision=mode)
    turned = jnp.stack(
        [
            section[0] * cos_twist + section[1] * sin_twist,
            section[1] * cos_twist - section[0] * sin_twist,
        ]
    )
    return jnp.einsum("qrgj,rnfj->qngf", two, turned, precision=mode)


def times(value, angle):
    re, im = value
    if angle % 16 == 0:
        return re, im
    c, s = math.cos(2.0 * math.pi * angle / 16), math.sin(2.0 * math.pi * angle / 16)
    if angle % 16 == 4:
        return im, -re
    return re * c + im * s, im * c - re * s


def four(x):
    plus = [x[0][i] + x[2][i] for i in range(2)]
    minus = [x[0][i] - x[2][i] for i in range(2)]
    plus_odd = [x[1][i] + x[3][i] for i in range(2)]
    minus_odd = [x[1][i] - x[3][i] for i in range(2)]
    return [
        (plus[0] + plus_odd[0], plus[1] + plus_odd[1]),
        (minus[0] + minus_odd[1], minus[1] - minus_odd[0]),
        (plus[0] - plus_odd[0], plus[1] - plus_odd[1]),
        (minus[0] - minus_odd[1], minus[1] + minus_odd[0]),
    ]


def sixteen(x):
    inner = [four([x[4 * a + b] for a in range(4)]) for b in range(4)]
    result = [None] * 16
    for c in range(4):
        ends = four([times(inner[b][c], b * c) for b in range(4)])
        for d in range(4):
            result[c + 4 * d] = ends[d]
    return result


def spectra_kernel(x_ref, taps_ref, cos_ref, sin_ref, high_ref, low_ref, out_ref, held, turned):
    time_count, block = x_ref.shape[1:3]
    taps, length = taps_ref.shape
    frames = x_ref.shape[3] // length
    spectra_count = time_count * frames
    second = length // radix_first
    depth = AVG * spectra_count

    def filter_section(k1, carry):
        at = pl.multiple_of(k1 * second, second)
        rows = [taps_ref[m : m + 1, pl.ds(at, second)] for m in range(taps)]
        for r in range(2):
            samples = []
            for t in range(spectra_count):
                place = pl.multiple_of(k1 * second + (t % frames) * length, second)
                samples.append(x_ref[r, t // frames, :, pl.ds(place, second)].astype(jnp.float32))
            filtered = []
            for t in range(spectra_count):
                total = rows[0] * samples[t]
                for m in range(1, min(taps, t + 1)):
                    total = total + rows[m] * samples[t - m]
                filtered.append(total)
            held[r, :, :, pl.ds(at, second)] = jnp.transpose(jnp.stack(filtered), (1, 0, 2))
        return carry

    lax.fori_loop(0, radix_first, filter_section, 0)

    def transform_station(s, carry):
        sections = [
            tuple(held[r, s, :, k1 * second : (k1 + 1) * second] for r in range(2))
            for k1 in range(radix_first)
        ]
        rows = []
        for f1, (re, im) in enumerate(sixteen(sections)):
            c, n = cos_ref[f1 : f1 + 1, :], sin_ref[f1 : f1 + 1, :]
            rows.append(jnp.concatenate([re * c + im * n, im * c - re * n], axis=-1))
        joined = jnp.concatenate(rows, axis=0)
        high = joined.astype(jnp.bfloat16)
        low = (joined - high.astype(jnp.float32)).astype(jnp.bfloat16)

        def product(matrix, data):
            return lax.dot_general(
                matrix, data, (((1,), (1,)), ((), ())), preferred_element_type=jnp.float32
            )

        turned[s] = (
            product(high_ref[...], high)
            + product(high_ref[...], low)
            + product(low_ref[...], high)
        )
        return carry

    lax.fori_loop(0, block, transform_station, 0)

    def place_channels(f, carry):
        at = pl.multiple_of(f * 16, 16)
        for q in range(2):
            for h in range(radix_first // AVG):
                part = turned[:, pl.ds(q * second + at, 16), h * depth : (h + 1) * depth]
                out_ref[pl.ds(at, 16), h, q] = jnp.transpose(part, (1, 0, 2)).astype(jnp.bfloat16)
        return carry

    lax.fori_loop(0, second // 16, place_channels, 0)


def local_spectra(blocks, taps_filter):
    _, time_count, share, samples = blocks.shape
    taps, length = taps_filter.shape
    spectra_count = time_count * (samples // length)
    second = length // radix_first
    depth = AVG * spectra_count
    block = 16
    inner = np.arange(second)
    twist = 2.0 * np.pi / length * (np.arange(radix_first)[:, None] * inner[None, :])
    phase = 2.0 * np.pi / second * (inner[:, None] * inner[None, :] % second)
    c, s = np.cos(phase) / math.sqrt(length), np.sin(phase) / math.sqrt(length)
    matrix = np.block([[c, s], [-s, c]])
    high = matrix.astype(ml_dtypes.bfloat16)
    low = (matrix - high.astype(np.float64)).astype(ml_dtypes.bfloat16)
    whole = lambda shape: pl.BlockSpec(shape, lambda i: (0, 0))
    return pl.pallas_call(
        spectra_kernel,
        grid=(share // block,),
        in_specs=[
            pl.BlockSpec((2, time_count, block, samples), lambda i: (0, 0, i, 0)),
            whole((taps, length)),
            whole((radix_first, second)),
            whole((radix_first, second)),
            whole((2 * second, 2 * second)),
            whole((2 * second, 2 * second)),
        ],
        out_specs=pl.BlockSpec(
            (second, radix_first // AVG, 2, block, depth), lambda i: (0, 0, 0, i, 0)
        ),
        out_shape=jax.ShapeDtypeStruct(
            (second, radix_first // AVG, 2, share, depth), jnp.bfloat16
        ),
        scratch_shapes=[
            pltpu.VMEM((2, block, spectra_count, length), jnp.float32),
            pltpu.VMEM((block, 2 * second, radix_first * spectra_count), jnp.float32),
        ],
        compiler_params=pltpu.CompilerParams(vmem_limit_bytes=48 * 2**20),
    )(
        blocks,
        taps_filter,
        np.cos(twist).astype(np.float32),
        np.sin(twist).astype(np.float32),
        high,
        low,
    )


def plain_spectra(blocks, taps_filter):
    _, time_count, share, samples = blocks.shape
    taps, length = taps_filter.shape
    frames = samples // length
    spectra_count = time_count * frames
    blocks = blocks.reshape(2, time_count, share, frames, length)
    blocks = blocks.transpose(0, 2, 1, 3, 4).reshape(2, share, spectra_count, length)
    extended = jnp.pad(blocks, ((0, 0), (0, 0), (taps - 1, 0), (0, 0)))
    filtered = jnp.zeros((2, share, spectra_count, length), jnp.float32)
    for tap_index in range(taps):
        start = taps - 1 - tap_index
        filtered = filtered + taps_filter[tap_index] * extended[
            :, :, start : start + spectra_count
        ].astype(jnp.float32)
    spectra = fourier(filtered.reshape(2, share * spectra_count, length)).astype(jnp.bfloat16)
    outgoing = spectra.reshape(
        2, share, spectra_count, length // radix_first, radix_first // AVG, AVG
    )
    return outgoing.transpose(3, 4, 0, 1, 5, 2).reshape(
        length // radix_first, radix_first // AVG, 2, share, AVG * spectra_count
    )


def correlate_kernel(rows_ref, weight_ref, full_ref, out_ref, pick):
    pols, sources, bands, parts, part_stations, depth = full_ref.shape
    stations = sources * part_stations
    capacity = out_ref.shape[0]
    width = out_ref.shape[4]

    @pl.when(pl.program_id(0) == 0)
    def _():
        columns = lax.broadcasted_iota(jnp.int32, pick.shape, 1)
        pick[...] = jnp.where(rows_ref[...] == columns, 1.0, 0.0).astype(jnp.bfloat16)

    for band in range(bands):
        source = jnp.concatenate(
            [
                full_ref[p, :, band, r].reshape(stations, depth)
                for p in range(2)
                for r in range(2)
            ],
            axis=-1,
        )
        picked = jnp.dot(pick[...], source, preferred_element_type=jnp.float32).astype(
            jnp.bfloat16
        )
        for slot in range(capacity):
            at = 2 * width * slot
            weight = weight_ref[slot]
            left = [
                picked[at : at + width, i * depth : (i + 1) * depth] * weight for i in range(4)
            ]
            other = picked[at + width : at + 2 * width]
            left_rows = jnp.concatenate(
                [
                    jnp.concatenate([left[0], left[1]], axis=-1),
                    jnp.concatenate([left[2], left[3]], axis=-1),
                    jnp.concatenate([left[1], -left[0]], axis=-1),
                    jnp.concatenate([left[3], -left[2]], axis=-1),
                ],
                axis=0,
            )
            right_rows = jnp.concatenate([other[:, : 2 * depth], other[:, 2 * depth :]], axis=0)
            result = lax.dot_general(
                left_rows,
                right_rows,
                (((1,), (1,)), ((), ())),
                preferred_element_type=jnp.float32,
            ) * (1.0 / depth)
            out_ref[slot, band] = result.reshape(2, 2, width, 2 * width)


def correlate(full, rows, weight):
    pols, sources, bands, parts, part_stations, depth = full.shape
    width = rows.shape[1] // 2
    step = 2 if bands % 2 == 0 and bands > 2 else 1
    return pl.pallas_call(
        correlate_kernel,
        grid=(bands // step,),
        in_specs=[
            pl.BlockSpec((CAP * 2 * width, 1), lambda g: (0, 0)),
            pl.BlockSpec((CAP, 1, depth), lambda g: (0, 0, 0)),
            pl.BlockSpec(
                (pols, sources, step, parts, part_stations, depth), lambda g: (0, 0, g, 0, 0, 0)
            ),
        ],
        out_specs=pl.BlockSpec(
            (CAP, step, 2, 2, width, 2 * width), lambda g: (0, g, 0, 0, 0, 0)
        ),
        out_shape=jax.ShapeDtypeStruct((CAP, bands, 2, 2, width, 2 * width), jnp.float32),
        scratch_shapes=[pltpu.VMEM((CAP * 2 * width, sources * part_stations), jnp.bfloat16)],
        compiler_params=pltpu.CompilerParams(vmem_limit_bytes=48 * 2**20),
    )(rows.reshape(CAP * 2 * width, 1), weight.astype(jnp.bfloat16), full)


def on_device(voltages, taps_filter, tile_a, tile_b, tile_owner, tile_flags):
    taps, length = taps_filter.shape
    stations = voltages.shape[2]
    frames = voltages.shape[3] // length
    chan_count = lax.axis_size("chan")
    time_count = lax.axis_size("tm")
    spectra_count = time_count * frames
    share = stations // time_count

    blocks = voltages.reshape(2, time_count, share, frames * length)
    blocks = lax.all_to_all(blocks, "tm", split_axis=1, concat_axis=1, tiled=True)
    spectra = (local_spectra if share % 16 == 0 else plain_spectra)(blocks, taps_filter)

    owners = chan_count * time_count
    bands = length // (owners * AVG)
    outgoing = spectra.reshape(owners, bands, 2, share, AVG * spectra_count)
    moved = lax.all_to_all(outgoing, ("chan", "tm"), split_axis=0, concat_axis=0, tiled=True)
    full = lax.all_gather(moved, "pol", axis=0)

    position = lax.axis_index("pol")
    held = tile_owner == position
    rank = jnp.cumsum(held.astype(jnp.int32)) - 1
    chosen = (
        (rank[None, :] == jnp.arange(CAP, dtype=jnp.int32)[:, None]) & held[None, :]
    ).astype(jnp.int32)
    pairs = jnp.concatenate([tile_a, tile_b], axis=1)
    rows = jnp.sum(chosen[:, :, None] * pairs[None], axis=1)[:, :, None]
    flags = jnp.sum(chosen[:, :, None] * tile_flags[None], axis=1)
    weight = jnp.tile(flags.astype(jnp.float32), (1, AVG))[:, None, :]
    return correlate(full, rows, weight)


def solution(mesh):
    return jax.shard_map(
        on_device,
        mesh=mesh,
        in_specs=(P("grp", "pol", "chan", "tm"), P(), P(), P(), P(), P()),
        out_specs=P("pol", ("chan", "tm"), "grp", None, None, None),
        check_vma=False,
    )
```

```python
import math

import jax
import ml_dtypes
import numpy as np
import jax.numpy as jnp
from jax import lax
from jax.experimental import pallas as pl
from jax.experimental.pallas import tpu as pltpu
from jax.sharding import PartitionSpec as P

AVG = 8
CAP = 8

radix_first = 16


def fourier(filtered):
    length = filtered.shape[-1]
    second = length // radix_first
    mode = lax.Precision.HIGH
    grid = filtered.reshape(filtered.shape[:-1] + (radix_first, second))
    outer = jnp.arange(radix_first, dtype=jnp.int32)
    inner = jnp.arange(second, dtype=jnp.int32)
    phase_one = (
        2.0
        * math.pi
        / radix_first
        * (outer[:, None] * outer[None, :] % radix_first).astype(jnp.float32)
    )
    phase_twist = 2.0 * math.pi / length * (outer[:, None] * inner[None, :]).astype(jnp.float32)
    phase_two = (
        2.0 * math.pi / second * (inner[:, None] * inner[None, :] % second).astype(jnp.float32)
    )
    scale = 1.0 / math.sqrt(length)
    cos_one, sin_one = (jnp.cos(phase_one), jnp.sin(phase_one))
    cos_twist, sin_twist = (jnp.cos(phase_twist), jnp.sin(phase_twist))
    cos_two, sin_two = (jnp.cos(phase_two) * scale, jnp.sin(phase_two) * scale)
    one = jnp.stack([jnp.stack([cos_one, sin_one]), jnp.stack([-sin_one, cos_one])])
    two = jnp.stack([jnp.stack([cos_two, sin_two]), jnp.stack([-sin_two, cos_two])])
    section = jnp.einsum("qrfk,rnkj->qnfj", one, grid, precision=mode)
    turned = jnp.stack(
        [
            section[0] * cos_twist + section[1] * sin_twist,
            section[1] * cos_twist - section[0] * sin_twist,
        ]
    )
    return jnp.einsum("qrgj,rnfj->qngf", two, turned, precision=mode)


def times(value, angle):
    re, im = value
    if angle % 16 == 0:
        return re, im
    c, s = math.cos(2.0 * math.pi * angle / 16), math.sin(2.0 * math.pi * angle / 16)
    if angle % 16 == 4:
        return im, -re
    return re * c + im * s, im * c - re * s


def four(x):
    plus = [x[0][i] + x[2][i] for i in range(2)]
    minus = [x[0][i] - x[2][i] for i in range(2)]
    plus_odd = [x[1][i] + x[3][i] for i in range(2)]
    minus_odd = [x[1][i] - x[3][i] for i in range(2)]
    return [
        (plus[0] + plus_odd[0], plus[1] + plus_odd[1]),
        (minus[0] + minus_odd[1], minus[1] - minus_odd[0]),
        (plus[0] - plus_odd[0], plus[1] - plus_odd[1]),
        (minus[0] - minus_odd[1], minus[1] + minus_odd[0]),
    ]


def sixteen(x):
    inner = [four([x[4 * a + b] for a in range(4)]) for b in range(4)]
    result = [None] * 16
    for c in range(4):
        ends = four([times(inner[b][c], b * c) for b in range(4)])
        for d in range(4):
            result[c + 4 * d] = ends[d]
    return result


def spectra_kernel(x_ref, taps_ref, cos_ref, sin_ref, high_ref, low_ref, out_ref, held, turned):
    time_count, block = x_ref.shape[1:3]
    taps, length = taps_ref.shape
    frames = x_ref.shape[3] // length
    spectra_count = time_count * frames
    second = length // radix_first
    depth = AVG * spectra_count

    def filter_section(k1, carry):
        at = pl.multiple_of(k1 * second, second)
        rows = [taps_ref[m : m + 1, pl.ds(at, second)] for m in range(taps)]
        for r in range(2):
            samples = []
            for t in range(spectra_count):
                place = pl.multiple_of(k1 * second + (t % frames) * length, second)
                samples.append(x_ref[r, t // frames, :, pl.ds(place, second)].astype(jnp.float32))
            filtered = []
            for t in range(spectra_count):
                total = rows[0] * samples[t]
                for m in range(1, min(taps, t + 1)):
                    total = total + rows[m] * samples[t - m]
                filtered.append(total)
            held[r, :, :, pl.ds(at, second)] = jnp.transpose(jnp.stack(filtered), (1, 0, 2))
        return carry

    lax.fori_loop(0, radix_first, filter_section, 0)

    def transform_station(s, carry):
        sections = [
            tuple(held[r, s, :, k1 * second : (k1 + 1) * second] for r in range(2))
            for k1 in range(radix_first)
        ]
        rows = []
        for f1, (re, im) in enumerate(sixteen(sections)):
            c, n = cos_ref[f1 : f1 + 1, :], sin_ref[f1 : f1 + 1, :]
            rows.append(jnp.concatenate([re * c + im * n, im * c - re * n], axis=-1))
        joined = jnp.concatenate(rows, axis=0)
        high = joined.astype(jnp.bfloat16)
        low = (joined - high.astype(jnp.float32)).astype(jnp.bfloat16)

        def product(matrix, data):
            return lax.dot_general(
                matrix, data, (((1,), (1,)), ((), ())), preferred_element_type=jnp.float32
            )

        turned[s] = (
            product(high_ref[...], high)
            + product(high_ref[...], low)
            + product(low_ref[...], high)
        )
        return carry

    lax.fori_loop(0, block, transform_station, 0)

    def place_channels(f, carry):
        at = pl.multiple_of(f * 16, 16)
        for q in range(2):
            for h in range(radix_first // AVG):
                part = turned[:, pl.ds(q * second + at, 16), h * depth : (h + 1) * depth]
                out_ref[pl.ds(at, 16), h, q] = jnp.transpose(part, (1, 0, 2)).astype(jnp.bfloat16)
        return carry

    lax.fori_loop(0, second // 16, place_channels, 0)


def local_spectra(blocks, taps_filter):
    _, time_count, share, samples = blocks.shape
    taps, length = taps_filter.shape
    spectra_count = time_count * (samples // length)
    second = length // radix_first
    depth = AVG * spectra_count
    block = 16
    inner = np.arange(second)
    twist = 2.0 * np.pi / length * (np.arange(radix_first)[:, None] * inner[None, :])
    phase = 2.0 * np.pi / second * (inner[:, None] * inner[None, :] % second)
    c, s = np.cos(phase) / math.sqrt(length), np.sin(phase) / math.sqrt(length)
    matrix = np.block([[c, s], [-s, c]])
    high = matrix.astype(ml_dtypes.bfloat16)
    low = (matrix - high.astype(np.float64)).astype(ml_dtypes.bfloat16)
    whole = lambda shape: pl.BlockSpec(shape, lambda i: (0, 0))
    return pl.pallas_call(
        spectra_kernel,
        grid=(share // block,),
        in_specs=[
            pl.BlockSpec((2, time_count, block, samples), lambda i: (0, 0, i, 0)),
            whole((taps, length)),
            whole((radix_first, second)),
            whole((radix_first, second)),
            whole((2 * second, 2 * second)),
            whole((2 * second, 2 * second)),
        ],
        out_specs=pl.BlockSpec(
            (second, radix_first // AVG, 2, block, depth), lambda i: (0, 0, 0, i, 0)
        ),
        out_shape=jax.ShapeDtypeStruct(
            (second, radix_first // AVG, 2, share, depth), jnp.bfloat16
        ),
        scratch_shapes=[
            pltpu.VMEM((2, block, spectra_count, length), jnp.float32),
            pltpu.VMEM((block, 2 * second, radix_first * spectra_count), jnp.float32),
        ],
        compiler_params=pltpu.CompilerParams(vmem_limit_bytes=48 * 2**20),
    )(
        blocks,
        taps_filter,
        np.cos(twist).astype(np.float32),
        np.sin(twist).astype(np.float32),
        high,
        low,
    )


def plain_spectra(blocks, taps_filter):
    _, time_count, share, samples = blocks.shape
    taps, length = taps_filter.shape
    frames = samples // length
    spectra_count = time_count * frames
    blocks = blocks.reshape(2, time_count, share, frames, length)
    blocks = blocks.transpose(0, 2, 1, 3, 4).reshape(2, share, spectra_count, length)
    extended = jnp.pad(blocks, ((0, 0), (0, 0), (taps - 1, 0), (0, 0)))
    filtered = jnp.zeros((2, share, spectra_count, length), jnp.float32)
    for tap_index in range(taps):
        start = taps - 1 - tap_index
        filtered = filtered + taps_filter[tap_index] * extended[
            :, :, start : start + spectra_count
        ].astype(jnp.float32)
    spectra = fourier(filtered.reshape(2, share * spectra_count, length)).astype(jnp.bfloat16)
    outgoing = spectra.reshape(
        2, share, spectra_count, length // radix_first, radix_first // AVG, AVG
    )
    return outgoing.transpose(3, 4, 0, 1, 5, 2).reshape(
        length // radix_first, radix_first // AVG, 2, share, AVG * spectra_count
    )


def correlate_kernel(place_ref, rows_ref, weight_ref, own_ref, other_ref, out_ref, pick, source):
    sources, bands, parts, part_stations, depth = own_ref.shape
    stations = sources * part_stations
    capacity = out_ref.shape[0]
    width = out_ref.shape[4]

    @pl.when(pl.program_id(0) == 0)
    def _():
        columns = lax.broadcasted_iota(jnp.int32, pick.shape, 1)
        pick[...] = jnp.where(rows_ref[...] == columns, 1.0, 0.0).astype(jnp.bfloat16)

    for band in range(bands):
        for ref, polarisation in ((own_ref, place_ref[0]), (other_ref, 1 - place_ref[0])):
            at = pl.multiple_of(polarisation * (2 * depth), depth)
            source[band, :, pl.ds(at, 2 * depth)] = jnp.concatenate(
                [ref[:, band, r].reshape(stations, depth) for r in range(2)], axis=-1
            )
        picked = jnp.dot(pick[...], source[band], preferred_element_type=jnp.float32).astype(
            jnp.bfloat16
        )
        for slot in range(capacity):
            at = 2 * width * slot
            weight = weight_ref[slot]
            left = [
                picked[at : at + width, i * depth : (i + 1) * depth] * weight for i in range(4)
            ]
            other = picked[at + width : at + 2 * width]
            left_rows = jnp.concatenate(
                [
                    jnp.concatenate([left[0], left[1]], axis=-1),
                    jnp.concatenate([left[2], left[3]], axis=-1),
                    jnp.concatenate([left[1], -left[0]], axis=-1),
                    jnp.concatenate([left[3], -left[2]], axis=-1),
                ],
                axis=0,
            )
            right_rows = jnp.concatenate([other[:, : 2 * depth], other[:, 2 * depth :]], axis=0)
            result = lax.dot_general(
                left_rows,
                right_rows,
                (((1,), (1,)), ((), ())),
                preferred_element_type=jnp.float32,
            ) * (1.0 / depth)
            out_ref[slot, band] = result.reshape(2, 2, width, 2 * width)


def correlate(place, own, other, rows, weight):
    sources, bands, parts, part_stations, depth = own.shape
    width = rows.shape[1] // 2
    step = 2 if bands % 2 == 0 and bands > 2 else 1
    return pl.pallas_call(
        correlate_kernel,
        grid=(bands // step,),
        in_specs=[
            pl.BlockSpec(memory_space=pltpu.SMEM),
            pl.BlockSpec((CAP * 2 * width, 1), lambda g: (0, 0)),
            pl.BlockSpec((CAP, 1, depth), lambda g: (0, 0, 0)),
            pl.BlockSpec((sources, step, parts, part_stations, depth), lambda g: (0, g, 0, 0, 0)),
            pl.BlockSpec((sources, step, parts, part_stations, depth), lambda g: (0, g, 0, 0, 0)),
        ],
        out_specs=pl.BlockSpec(
            (CAP, step, 2, 2, width, 2 * width), lambda g: (0, g, 0, 0, 0, 0)
        ),
        out_shape=jax.ShapeDtypeStruct((CAP, bands, 2, 2, width, 2 * width), jnp.float32),
        scratch_shapes=[
            pltpu.VMEM((CAP * 2 * width, sources * part_stations), jnp.bfloat16),
            pltpu.VMEM((step, sources * part_stations, 4 * depth), jnp.bfloat16),
        ],
        compiler_params=pltpu.CompilerParams(vmem_limit_bytes=48 * 2**20),
    )(place, rows.reshape(CAP * 2 * width, 1), weight.astype(jnp.bfloat16), own, other)


def on_device(voltages, taps_filter, tile_a, tile_b, tile_owner, tile_flags):
    taps, length = taps_filter.shape
    stations = voltages.shape[2]
    frames = voltages.shape[3] // length
    chan_count = lax.axis_size("chan")
    time_count = lax.axis_size("tm")
    spectra_count = time_count * frames
    share = stations // time_count

    blocks = voltages.reshape(2, time_count, share, frames * length)
    blocks = lax.all_to_all(blocks, "tm", split_axis=1, concat_axis=1, tiled=True)
    spectra = (local_spectra if share % 16 == 0 else plain_spectra)(blocks, taps_filter)

    owners = chan_count * time_count
    bands = length // (owners * AVG)
    outgoing = spectra.reshape(owners, bands, 2, share, AVG * spectra_count)
    moved = lax.all_to_all(outgoing, ("chan", "tm"), split_axis=0, concat_axis=0, tiled=True)
    other = lax.ppermute(moved, "pol", [(0, 1), (1, 0)])

    position = lax.axis_index("pol")
    held = tile_owner == position
    rank = jnp.cumsum(held.astype(jnp.int32)) - 1
    chosen = (
        (rank[None, :] == jnp.arange(CAP, dtype=jnp.int32)[:, None]) & held[None, :]
    ).astype(jnp.int32)
    pairs = jnp.concatenate([tile_a, tile_b], axis=1)
    rows = jnp.sum(chosen[:, :, None] * pairs[None], axis=1)[:, :, None]
    flags = jnp.sum(chosen[:, :, None] * tile_flags[None], axis=1)
    weight = jnp.tile(flags.astype(jnp.float32), (1, AVG))[:, None, :]
    return correlate(position.reshape(1).astype(jnp.int32), moved, other, rows, weight)


def solution(mesh):
    return jax.shard_map(
        on_device,
        mesh=mesh,
        in_specs=(P("grp", "pol", "chan", "tm"), P(), P(), P(), P(), P()),
        out_specs=P("pol", ("chan", "tm"), "grp", None, None, None),
        check_vma=False,
    )
```
